32 devices in a mesh: dp: 8 (over z, y), expert: 4 (over x, core).
Axes of the slice: x: 2, y: 2, z: 4, core: 2. Of those that a mesh axis runs over, the one named last changes fastest.
Arguments:
- master: float32 [4, 4096, 1536], P('expert', 'dp'), may hold values from -0.109375 to 0.109375
- moment_one: float32 [4, 4096, 1536], P('expert', 'dp'), may hold values from -1.5 to 1.5
- moment_two: float32 [4, 4096, 1536], P('expert', 'dp'), may hold values from 0.0001 to 0.003
- saved_rows: bfloat16 [4, 3072, 1536], P('expert', 'dp'), may hold values from -6 to 6
- saved_grads: bfloat16 [4, 3072, 4096], P('expert', 'dp'), may hold values from -0.15625 to 0.15625
- slot_rows: bfloat16 [4096, 2, 1536], P(('dp', 'expert')), may hold values from -6 to 6
- routes: int32 [4096, 2], P(('dp', 'expert')), may hold values from 0 to 3, all different within a row; in each aligned block of 128 rows (0 to 127, 128 to 255, ...) at most 80 rows name the same one
- gates: float32 [4096, 2], P(('dp', 'expert')), may hold values from 0.1 to 1
Outputs:
- master_new: float32 [4, 4096, 1536], P('expert', 'dp')
- moment_one_new: float32 [4, 4096, 1536], P('expert', 'dp')
- moment_two_new: float32 [4, 4096, 1536], P('expert', 'dp')
- mixed: bfloat16 [4096, 4096], P(('dp', 'expert'))
The draws below stay inside these ranges and needn't reach their ends.
Inputs may be any that keep to these rules, and one draw needn't show every extreme that they name: `routes`: each token names 2 different experts. Among the 128 tokens of one device (aligned blocks of rows in device order, dp slowest) at most 80 name the same expert, and in some device's block exactly 80 do.
All inputs are finite; a program needn't handle non-finite values.
Results may differ from the reference program's by a relative error of at most 0.034.
Values may be sent and summed in bfloat16 or wider, within the bound.
A program may use at most 128 MiB of HBM per device.

```python
import math
import jax
import jax.numpy as jnp
import numpy as np
from jax import lax

D = 4096
FF = 1536
TOPK = 2
TOK_DEV = 128
SAVED = 384
EXPERTS = 4
CAP = 80
TOKENS = 4096
N_DP = 8


def strengthened(entries, rng, source, target, parts, factor):
    owner, partner = [(jnp.arange(entries.shape[dim]) // (entries.shape[dim] // parts)).reshape([-1 if axis == dim else 1 for axis in range(entries.ndim)]) for dim in (source, target)]
    chosen = jax.random.permutation(rng, parts)[partner]
    strong = (owner == chosen) | (owner == (partner + parts // 2) % parts)
    return jnp.where(strong, factor * entries, entries)


def block_scale(own_key, extent, pieces, least, largest):
    factor_of, own = 1.0, jax.random.fold_in(own_key, 6)
    for position, shards_of in pieces:
        steps = jnp.exp(jax.random.uniform(jax.random.fold_in(own, position), (shards_of,), jnp.float32, least / len(pieces), largest / len(pieces)))
        factor_of = factor_of * jnp.repeat(steps, extent[position] // shards_of).reshape([-1 if axis == position else 1 for axis in range(len(extent))])
    return factor_of


def deal_out(rng, own, number, rows, amount, top, most, lean):
    sequence = jax.random.permutation(rng, amount)
    heavy_load, usual = load_shares(amount, rows * top, most, lean, True), load_shares(amount, rows * top, most, lean, False)
    places = jnp.arange(amount)

    def named(lengths, offset_by):
        used = int((lengths > 0).sum())
        fixed = max(1, used // 4)
        moved = fixed + (places - fixed + offset_by * (used - fixed)) % max(1, amount - fixed)
        return jnp.zeros((amount,), jnp.int32).at[sequence[jnp.where(places < fixed, places, moved)]].set(jnp.asarray(lengths, jnp.int32))

    lengths = jnp.where(number % 4 == 0, named(heavy_load, number // 4), named(usual, number - number // 4 - 1))
    mixed = jax.random.permutation(jax.random.fold_in(own, 3), amount)
    source_of, taker = mixed[0:amount // 2 * 2:2], mixed[1:amount // 2 * 2:2]
    slack = jnp.minimum(lengths[source_of] - 1, most - lengths[taker]) // 2
    slack = jnp.where((source_of == sequence[0]) | (taker == sequence[0]) | (lengths[taker] == 0), 0, jnp.maximum(slack, 0))
    moved = jax.random.randint(jax.random.fold_in(own, 4), (amount // 2,), 0, 1 << 20) % (slack + 1)
    lengths = lengths.at[source_of].add(-moved).at[taker].add(moved)
    members = jnp.searchsorted(jnp.cumsum(lengths), jnp.arange(rows * top), side="right").astype(jnp.int32)
    listing = members.reshape(top, rows).T
    listing = listing[jax.random.permutation(jax.random.fold_in(own, 1), rows)]
    offset_by = jax.random.randint(jax.random.fold_in(own, 2), (rows, 1), 0, top)
    return jnp.take_along_axis(listing, (jnp.arange(top)[None, :] + offset_by) % top, axis=1)


def load_shares(number_of, total, most, lean, full):
    weights = [(1 << 20) // math.isqrt(rank ** lean) + 1 for rank in range(1, number_of + 1)]
    largest = most if full else min(most, max(-(-total // number_of), total * weights[0] // sum(weights)))
    least = 1 if total - largest >= number_of - 1 else 0
    holding, surplus = [largest] + [least] * (number_of - 1), total - largest - least * (number_of - 1)
    while surplus > 0:
        candidates = [i for i in range(1, number_of) if holding[i] < largest] or [i for i in range(1, number_of) if holding[i] < most]
        pool, budget = sum([weights[i] for i in candidates]), surplus
        for i in candidates:
            extra = min(most - holding[i], max(1, budget * weights[i] // pool), surplus)
            holding[i] = holding[i] + extra
            surplus = surplus - extra
    return np.array(holding)


def gaussian(key, dims, deviation, reach, split=(), kind=jnp.bfloat16):
    drawn = deviation * jax.random.normal(key, dims, jnp.float32)
    if split:
        drawn = drawn * block_scale(key, dims, split, -0.22, 0.18)
    return jnp.clip(drawn, -reach, reach).astype(kind)


def noise_with(rng, dims, scale, limit, pieces, heavy, kind=jnp.bfloat16):
    entries = scale * jax.random.normal(rng, dims, jnp.float32)
    if pieces:
        entries = entries * block_scale(rng, dims, pieces, -0.22, 0.18)
    return jnp.clip(strengthened(entries, jax.random.fold_in(rng, 3), *heavy), -limit, limit).astype(kind)


def setup_inputs(seed: int = 0) -> dict:
    key_list = jax.random.split(jax.random.key(seed), 9)
    master = gaussian(key_list[0], (EXPERTS, D, FF), (2 * FF) ** -0.5, 0.109375, ((0, 4), (1, 8)), jnp.float32)
    moment_one = gaussian(key_list[1], (EXPERTS, D, FF), 0.1, 1.5, ((0, 4), (1, 8)), jnp.float32)
    moment_two = jnp.clip(jnp.exp(math.log(0.003) - 3.4011974 * jax.random.uniform(key_list[2], (EXPERTS, D, FF), jnp.float32) ** block_scale(key_list[2], (EXPERTS, D, FF), ((0, 4), (1, 8)), -0.2, 0.2)), 0.0001, 0.003)
    saved_rows = gaussian(key_list[3], (EXPERTS, SAVED * N_DP, FF), 1.0, 6.0, ((0, 4), (1, 8)))
    saved_grads = noise_with(key_list[4], (EXPERTS, SAVED * N_DP, D), (SAVED * N_DP) ** -0.5, 0.15625, ((0, 4), (1, 8)), (1, 2, 8, 2.0))
    slot_rows = gaussian(key_list[5], (TOKENS, TOPK, FF), 1.0, 6.0, ((0, 32),))
    routes_keys = jax.random.split(jax.random.fold_in(key_list[6], 1), TOKENS // TOK_DEV)
    routes_turns = jax.random.permutation(jax.random.fold_in(key_list[6], 3), TOKENS // TOK_DEV)
    routes = jax.vmap(lambda own, number: deal_out(jax.random.fold_in(key_list[6], 2), own, number, TOK_DEV, EXPERTS, TOPK, CAP, 2))(routes_keys, routes_turns).reshape((TOKENS, TOPK))
    gates = jnp.clip(0.1 + 0.9 * jax.random.uniform(key_list[7], (TOKENS, TOPK), jnp.float32) ** block_scale(key_list[7], (TOKENS, TOPK), ((0, 32),), -0.2, 0.2), 0.1, 1.0)
    return dict(master=master, moment_one=moment_one, moment_two=moment_two, saved_rows=saved_rows, saved_grads=saved_grads, slot_rows=slot_rows, routes=routes, gates=gates)


beta_one = 0.9
beta_two = 0.999
learn_rate = 0.002
tiny_eps = 1e-08
steps_done = 100.0

def adam_update(master, moment_one, moment_two, grad):
    m_new = beta_one * moment_one + (1.0 - beta_one) * grad
    v_new = beta_two * moment_two + (1.0 - beta_two) * grad * grad
    fix_one = 1.0 - beta_one ** steps_done
    fix_two = 1.0 - beta_two ** steps_done
    step_size = m_new / fix_one / (jnp.sqrt(v_new / fix_two) + tiny_eps)
    return (master - learn_rate * step_size, m_new, v_new)

def reference(master, moment_one, moment_two, saved_rows, saved_grads, slot_rows, routes, gates):

    def expert_grad(pair):
        rows = pair[0].reshape(N_DP, SAVED, FF)
        grads = pair[1].reshape(N_DP, SAVED, D)

        def add_part(total, piece):
            part = lax.dot_general(piece[1], piece[0], (((0,), (0,)), ((), ())), preferred_element_type=jnp.float32)
            part = lax.optimization_barrier(part.astype(jnp.bfloat16))
            return (total + part.astype(jnp.float32), None)
        total, _ = lax.scan(add_part, jnp.zeros((D, FF), jnp.float32), (rows, grads))
        return total
    grad = lax.map(expert_grad, (saved_rows, saved_grads))
    master_new, m_new, v_new = adam_update(master, moment_one, moment_two, grad)
    weights = master_new.astype(jnp.bfloat16)
    blocks = TOKENS // TOK_DEV
    width = TOK_DEV * TOPK
    flat = routes.reshape(blocks, width).astype(jnp.int32)
    onehot = (flat[:, :, None] == jnp.arange(EXPERTS, dtype=jnp.int32)[None, None, :]).astype(jnp.int32)
    place = lax.optimization_barrier(jnp.sum((jnp.cumsum(onehot, axis=1) - onehot) * onehot, axis=2)).astype(jnp.int32)
    rows_all = slot_rows.reshape(blocks, width, FF)
    block_ids = jnp.broadcast_to(jnp.arange(blocks, dtype=jnp.int32)[:, None], (blocks, width))

    def expert_out(pair):
        expert_id, weight = pair
        index = jnp.where(flat == expert_id, place, CAP).astype(jnp.int32)
        table = jnp.zeros((blocks, CAP + 1, FF), jnp.bfloat16).at[block_ids, index].set(rows_all)
        outs = lax.dot_general(table[:, :CAP].reshape(blocks * CAP, FF), weight, (((1,), (1,)), ((), ())), preferred_element_type=jnp.float32)
        return outs.astype(jnp.bfloat16).reshape(blocks, CAP, D)
    served = lax.map(expert_out, (jnp.arange(EXPERTS, dtype=jnp.int32), weights))

    def block_mix(item):
        block_id, experts_here, places_here, gate_here = item
        picked = served[experts_here, block_id, places_here].astype(jnp.float32)
        picked = picked.reshape(TOK_DEV, TOPK, D) * gate_here.reshape(TOK_DEV, TOPK)[:, :, None]
        return lax.optimization_barrier(jnp.sum(picked, axis=1)).astype(jnp.bfloat16)
    mixed = lax.map(block_mix, (jnp.arange(blocks, dtype=jnp.int32), flat, place, gates.reshape(blocks, width)))
    return (master_new, m_new, v_new, mixed.reshape(TOKENS, D))
```

```python
import functools

import jax
import jax.numpy as jnp
from jax import lax
from jax.experimental import pallas as pl
from jax.experimental.pallas import tpu as pltpu
from jax.sharding import PartitionSpec as P

beta_one = 0.9
beta_two = 0.999
learn_rate = 0.002
tiny_eps = 1e-08
steps_done = 100.0

MESH = pl.DeviceIdType.MESH


def adam_update(master, moment_one, moment_two, grad):
    m_new = beta_one * moment_one + (1.0 - beta_one) * grad
    v_new = beta_two * moment_two + (1.0 - beta_two) * grad * grad
    fix_one = 1.0 - beta_one**steps_done
    fix_two = 1.0 - beta_two**steps_done
    step_size = m_new / fix_one / (jnp.sqrt(v_new / fix_two) + tiny_eps)
    return (master - learn_rate * step_size, m_new, v_new)


def lanes_of(shard):
    if shard % 512 == 0:
        part = shard // 4
        return ((1, 0, part), (-1, part, part), (1, 2 * part, part), (-1, 3 * part, part))
    return ((1, 0, shard),)


def ring_place(index, n):
    return jnp.where(lax.rem(index, 2) == 0, index // 2, (2 * n - 1 - index) // 2)


def ring_index(place, n):
    place = lax.rem(place + 2 * n, n)
    return jnp.where(place < n // 2, 2 * place, 2 * n - 1 - 2 * place)


def greet(n, experts, here, expert):
    barrier = pltpu.get_barrier_semaphore()
    for step in (1, -1):
        pl.semaphore_signal(
            barrier, inc=1, device_id={"dp": ring_index(here + step, n)}, device_id_type=MESH
        )
    for other in range(1, experts):
        pl.semaphore_signal(
            barrier,
            inc=1,
            device_id={"expert": lax.rem(expert + other, experts)},
            device_id_type=MESH,
        )
    pl.semaphore_wait(barrier, experts + 1)


def reduce_kernel(
    n, experts, shard,
    rows_ref, grads_ref, out_ref, total_ref, got_ref,
    first, slots, part, send_sem, recv_sem, tok_send, tok_recv, own_sem,
):
    here = ring_place(lax.axis_index("dp"), n)
    expert = lax.axis_index("expert")
    lanes = lanes_of(shard)

    def partial(place, low, size):
        at = pl.multiple_of(ring_index(place, n) * shard + low, size)
        return lax.dot_general(
            grads_ref[:, pl.ds(at, size)],
            rows_ref[...],
            (((0,), (0,)), ((), ())),
            preferred_element_type=jnp.float32,
        )

    def send(step, lane, source):
        way, low, size = lanes[lane]
        return pltpu.make_async_remote_copy(
            src_ref=source.at[pl.ds(low, size)],
            dst_ref=slots.at[step, pl.ds(low, size)],
            send_sem=send_sem.at[step, lane],
            recv_sem=recv_sem.at[step, lane],
            device_id={"dp": ring_index(here + way, n)},
            device_id_type=MESH,
        )

    def token_copy(other):
        peer = lax.rem(expert + other, experts)
        return pltpu.make_async_remote_copy(
            src_ref=out_ref.at[peer],
            dst_ref=got_ref.at[expert],
            send_sem=tok_send.at[other],
            recv_sem=tok_recv.at[other],
            device_id={"expert": peer},
            device_id_type=MESH,
        )

    greet(n, experts, here, expert)
    for lane, (way, low, size) in enumerate(lanes):
        first[pl.ds(low, size)] = partial(here - way, low, size).astype(jnp.bfloat16)
        send(0, lane, first).start()
    for other in range(1, experts):
        token_copy(other).start()
    own = pltpu.make_async_copy(out_ref.at[expert], got_ref.at[expert], own_sem)
    own.start()

    def step_on(step, _):
        for lane, (way, low, size) in enumerate(lanes):
            part[pl.ds(low, size)] = partial(here - way * (2 + step), low, size)
            send(step, lane, first).wait_recv()
            slots[step, pl.ds(low, size)] = (
                slots[step, pl.ds(low, size)].astype(jnp.float32) + part[pl.ds(low, size)]
            ).astype(jnp.bfloat16)
            send(step + 1, lane, slots.at[step]).start()
        return 0

    lax.fori_loop(0, n - 2, step_on, 0)
    last = n - 2
    for lane, (way, low, size) in enumerate(lanes):
        part[pl.ds(low, size)] = partial(here, low, size)
    for lane, (way, low, size) in enumerate(lanes):
        send(last, lane, first).wait_recv()
        total_ref[pl.ds(low, size)] = (
            slots[last, pl.ds(low, size)].astype(jnp.float32) + part[pl.ds(low, size)]
        )

    def drain(step, _):
        for lane in range(len(lanes)):
            send(step, lane, first).wait_send()
        return 0

    lax.fori_loop(0, n - 1, drain, 0)
    for other in range(1, experts):
        token_copy(other).wait()
    own.wait()


def reduce_grad(n, experts, rows, grads, outgoing):
    saved, width = rows.shape
    depth = grads.shape[1]
    shard = depth // n
    lanes = len(lanes_of(shard))
    return pl.pallas_call(
        functools.partial(reduce_kernel, n, experts, shard),
        out_shape=(
            jax.ShapeDtypeStruct((shard, width), jnp.float32),
            jax.ShapeDtypeStruct(outgoing.shape, jnp.bfloat16),
        ),
        in_specs=[pl.BlockSpec(memory_space=pltpu.VMEM)] * 3,
        out_specs=(pl.BlockSpec(memory_space=pltpu.VMEM),) * 2,
        scratch_shapes=[
            pltpu.VMEM((shard, width), jnp.bfloat16),
            pltpu.VMEM((n - 1, shard, width), jnp.bfloat16),
            pltpu.VMEM((shard, width), jnp.float32),
            pltpu.SemaphoreType.DMA((n - 1, lanes)),
            pltpu.SemaphoreType.DMA((n - 1, lanes)),
            pltpu.SemaphoreType.DMA((experts,)),
            pltpu.SemaphoreType.DMA((experts,)),
            pltpu.SemaphoreType.DMA,
        ],
        compiler_params=pltpu.CompilerParams(
            collective_id=0, has_side_effects=True, vmem_limit_bytes=48 * 2**20
        ),
        cost_estimate=pl.CostEstimate(
            flops=2 * saved * width * depth, bytes_accessed=4 * depth * width, transcendentals=0
        ),
        name="reduce_grad",
    )(rows, grads, outgoing)


def product_kernel(
    n, experts, shard,
    weight_ref, tok_ref, back_ref,
    held, prod, send_sem, recv_sem, back_send, back_recv, own_sem,
):
    here = ring_place(lax.axis_index("dp"), n)
    expert = lax.axis_index("expert")
    lanes = lanes_of(shard)
    count = tok_ref.shape[0] // experts
    width = tok_ref.shape[1]

    def send(step, lane, source):
        way, low, size = lanes[lane]
        return pltpu.make_async_remote_copy(
            src_ref=source.at[pl.ds(low, size)],
            dst_ref=held.at[step, pl.ds(low, size)],
            send_sem=send_sem.at[step, lane],
            recv_sem=recv_sem.at[step, lane],
            device_id={"dp": ring_index(here + way, n)},
            device_id_type=MESH,
        )

    def back_copy(other, columns):
        peer = lax.rem(expert + other, experts)
        return pltpu.make_async_remote_copy(
            src_ref=prod.at[peer, :, columns],
            dst_ref=back_ref.at[expert, :, columns],
            send_sem=back_send.at[other],
            recv_sem=back_recv.at[other],
            device_id={"expert": peer},
            device_id_type=MESH,
        )

    def multiply(block, place, low, size):
        at = pl.multiple_of(ring_index(place, n) * shard + low, size)
        columns = pl.ds(at, size)
        out = lax.dot_general(
            tok_ref[...], block, (((1,), (1,)), ((), ())), preferred_element_type=jnp.float32
        )
        prod[:, :, columns] = out.astype(jnp.bfloat16).reshape(experts, count, size)
        for other in range(1, experts):
            back_copy(other, columns).start()
        pltpu.make_async_copy(
            prod.at[expert, :, columns], back_ref.at[expert, :, columns], own_sem
        ).start()

    greet(n, experts, here, expert)
    for lane in range(len(lanes)):
        send(0, lane, weight_ref).start()
    for way, low, size in lanes:
        multiply(weight_ref[pl.ds(low, size)], here, low, size)

    def step_on(step, _):
        for lane, (way, low, size) in enumerate(lanes):
            send(step, lane, weight_ref).wait_recv()

            @pl.when(step < n - 2)
            def _():
                send(step + 1, lane, held.at[step]).start()

            multiply(held[step, pl.ds(low, size)], here - way * (1 + step), low, size)
        return 0

    lax.fori_loop(0, n - 1, step_on, 0)

    def drain(step, _):
        for lane in range(len(lanes)):
            send(step, lane, weight_ref).wait_send()
        return 0

    lax.fori_loop(0, n - 1, drain, 0)
    for other in range(1, experts):
        back_copy(other, pl.ds(0, prod.shape[2])).wait()
    pltpu.make_async_copy(prod.at[expert], back_ref.at[expert], own_sem).wait()


def expert_product(n, experts, weights, tokens):
    shard, width = weights.shape
    depth = shard * n
    rows = tokens.shape[0]
    lanes = len(lanes_of(shard))
    return pl.pallas_call(
        functools.partial(product_kernel, n, experts, shard),
        out_shape=jax.ShapeDtypeStruct((experts, rows // experts, depth), jnp.bfloat16),
        in_specs=[pl.BlockSpec(memory_space=pltpu.VMEM)] * 2,
        out_specs=pl.BlockSpec(memory_space=pltpu.VMEM),
        scratch_shapes=[
            pltpu.VMEM((n - 1, shard, width), jnp.bfloat16),
            pltpu.VMEM((experts, rows // experts, depth), jnp.bfloat16),
            pltpu.SemaphoreType.DMA((n - 1, lanes)),
            pltpu.SemaphoreType.DMA((n - 1, lanes)),
            pltpu.SemaphoreType.DMA((experts,)),
            pltpu.SemaphoreType.DMA((experts,)),
            pltpu.SemaphoreType.DMA,
        ],
        compiler_params=pltpu.CompilerParams(
            collective_id=1, has_side_effects=True, vmem_limit_bytes=48 * 2**20
        ),
        cost_estimate=pl.CostEstimate(
            flops=2 * rows * width * depth, bytes_accessed=4 * depth * width, transcendentals=0
        ),
        name="expert_product",
    )(weights, tokens)


def body(n, master, moment_one, moment_two, saved_rows, saved_grads, slot_rows, routes, gates):
    experts = lax.axis_size("expert")
    tok_count, top_count, width = slot_rows.shape
    capacity = tok_count * top_count * 5 // (4 * experts)
    capacity = -(-capacity // 16) * 16
    flat = routes.reshape(-1)
    turn = jnp.arange(flat.shape[0], dtype=jnp.int32)
    same = (flat[:, None] == flat[None, :]) & (turn[None, :] < turn[:, None])
    slot = flat * capacity + jnp.sum(same.astype(jnp.int32), axis=1)
    places = jnp.arange(experts * capacity, dtype=jnp.int32)
    pick = (places[:, None] == slot[None, :]).astype(jnp.bfloat16)
    outgoing = (
        jnp.dot(pick, slot_rows.reshape(-1, width), preferred_element_type=jnp.float32)
        .astype(jnp.bfloat16)
        .reshape(experts, capacity, width)
    )
    grad, received = reduce_grad(n, experts, saved_rows[0], saved_grads[0], outgoing)
    master_new, m_new, v_new = adam_update(master[0], moment_one[0], moment_two[0], grad)
    returned = expert_product(
        n, experts, master_new.astype(jnp.bfloat16), received.reshape(-1, width)
    ).reshape(experts * capacity, -1)
    slot = slot.reshape(tok_count, top_count)
    share = jnp.sum(
        jnp.where(slot[:, :, None] == places[None, None, :], gates[:, :, None], 0.0), axis=1
    )
    high = share.astype(jnp.bfloat16)
    low = (share - high.astype(jnp.float32)).astype(jnp.bfloat16)
    mixed = jnp.dot(high, returned, preferred_element_type=jnp.float32) + jnp.dot(
        low, returned, preferred_element_type=jnp.float32
    )
    return (master_new[None], m_new[None], v_new[None], mixed.astype(jnp.bfloat16))


def solution(mesh):
    placed = (
        P("expert", "dp", None),
        P("expert", "dp", None),
        P("expert", "dp", None),
        P("expert", "dp", None),
        P("expert", "dp", None),
        P(("dp", "expert"), None, None),
        P(("dp", "expert"), None),
        P(("dp", "expert"), None),
    )
    return jax.shard_map(
        functools.partial(body, mesh.shape["dp"]),
        mesh=mesh,
        in_specs=placed,
        out_specs=(
            P("expert", "dp", None),
            P("expert", "dp", None),
            P("expert", "dp", None),
            P(("dp", "expert"), None),
        ),
        check_vma=False,
    )
```

```python
import functools

import jax
import jax.numpy as jnp
from jax import lax
from jax.experimental import pallas as pl
from jax.experimental.pallas import tpu as pltpu
from jax.sharding import PartitionSpec as P

beta_one = 0.9
beta_two = 0.999
learn_rate = 0.002
tiny_eps = 1e-08
steps_done = 100.0

MESH = pl.DeviceIdType.MESH


def adam_update(master, moment_one, moment_two, grad):
    m_new = beta_one * moment_one + (1.0 - beta_one) * grad
    v_new = beta_two * moment_two + (1.0 - beta_two) * grad * grad
    fix_one = 1.0 - beta_one**steps_done
    fix_two = 1.0 - beta_two**steps_done
    step_size = m_new / fix_one / (jnp.sqrt(v_new / fix_two) + tiny_eps)
    return (master - learn_rate * step_size, m_new, v_new)


def lanes_of(shard):
    if shard % 512 == 0:
        part = shard // 4
        return ((1, 0, part), (-1, part, part), (1, 2 * part, part), (-1, 3 * part, part))
    return ((1, 0, shard),)


def ring_place(index, n):
    return jnp.where(lax.rem(index, 2) == 0, index // 2, (2 * n - 1 - index) // 2)


def ring_index(place, n):
    place = lax.rem(place + 2 * n, n)
    return jnp.where(place < n // 2, 2 * place, 2 * n - 1 - 2 * place)


def greet(n, experts, here, expert):
    barrier = pltpu.get_barrier_semaphore()
    for step in (1, -1):
        pl.semaphore_signal(
            barrier, inc=1, device_id={"dp": ring_index(here + step, n)}, device_id_type=MESH
        )
    for other in range(1, experts):
        pl.semaphore_signal(
            barrier,
            inc=1,
            device_id={"expert": lax.rem(expert + other, experts)},
            device_id_type=MESH,
        )
    pl.semaphore_wait(barrier, experts + 1)


def reduce_kernel(
    n, experts, shard,
    rows_ref, grads_ref, out_ref, total_ref, got_ref,
    first, slots, part, send_sem, recv_sem, tok_send, tok_recv, own_sem,
):
    here = ring_place(lax.axis_index("dp"), n)
    expert = lax.axis_index("expert")
    lanes = lanes_of(shard)

    def partial(place, low, size):
        at = pl.multiple_of(ring_index(place, n) * shard + low, size)
        return lax.dot_general(
            grads_ref[:, pl.ds(at, size)],
            rows_ref[...],
            (((0,), (0,)), ((), ())),
            preferred_element_type=jnp.float32,
        )

    def send(step, lane, source):
        way, low, size = lanes[lane]
        return pltpu.make_async_remote_copy(
            src_ref=source.at[pl.ds(low, size)],
            dst_ref=slots.at[step, pl.ds(low, size)],
            send_sem=send_sem.at[step, lane],
            recv_sem=recv_sem.at[step, lane],
            device_id={"dp": ring_index(here + way, n)},
            device_id_type=MESH,
        )

    def token_copy(other):
        peer = lax.rem(expert + other, experts)
        return pltpu.make_async_remote_copy(
            src_ref=out_ref.at[peer],
            dst_ref=got_ref.at[expert],
            send_sem=tok_send.at[other],
            recv_sem=tok_recv.at[other],
            device_id={"expert": peer},
            device_id_type=MESH,
        )

    greet(n, experts, here, expert)
    for lane, (way, low, size) in enumerate(lanes):
        first[pl.ds(low, size)] = partial(here - way, low, size).astype(jnp.bfloat16)
        send(0, lane, first).start()
    for other in range(1, experts):
        token_copy(other).start()
    own = pltpu.make_async_copy(out_ref.at[expert], got_ref.at[expert], own_sem)
    own.start()

    def step_on(step, _):
        for lane, (way, low, size) in enumerate(lanes):
            part[pl.ds(low, size)] = partial(here - way * (2 + step), low, size)
            send(step, lane, first).wait_recv()
            slots[step, pl.ds(low, size)] = (
                slots[step, pl.ds(low, size)].astype(jnp.float32) + part[pl.ds(low, size)]
            ).astype(jnp.bfloat16)
            send(step + 1, lane, slots.at[step]).start()
        return 0

    lax.fori_loop(0, n - 2, step_on, 0)
    last = n - 2
    for lane, (way, low, size) in enumerate(lanes):
        part[pl.ds(low, size)] = partial(here, low, size)
    for lane, (way, low, size) in enumerate(lanes):
        send(last, lane, first).wait_recv()
        total_ref[pl.ds(low, size)] = (
            slots[last, pl.ds(low, size)].astype(jnp.float32) + part[pl.ds(low, size)]
        )

    def drain(step, _):
        for lane in range(len(lanes)):
            send(step, lane, first).wait_send()
        return 0

    lax.fori_loop(0, n - 1, drain, 0)
    for other in range(1, experts):
        token_copy(other).wait()
    own.wait()


def reduce_grad(n, experts, rows, grads, outgoing):
    saved, width = rows.shape
    depth = grads.shape[1]
    shard = depth // n
    lanes = len(lanes_of(shard))
    return pl.pallas_call(
        functools.partial(reduce_kernel, n, experts, shard),
        out_shape=(
            jax.ShapeDtypeStruct((shard, width), jnp.float32),
            jax.ShapeDtypeStruct(outgoing.shape, jnp.bfloat16),
        ),
        in_specs=[pl.BlockSpec(memory_space=pltpu.VMEM)] * 3,
        out_specs=(pl.BlockSpec(memory_space=pltpu.VMEM),) * 2,
        scratch_shapes=[
            pltpu.VMEM((shard, width), jnp.bfloat16),
            pltpu.VMEM((n - 1, shard, width), jnp.bfloat16),
            pltpu.VMEM((shard, width), jnp.float32),
            pltpu.SemaphoreType.DMA((n - 1, lanes)),
            pltpu.SemaphoreType.DMA((n - 1, lanes)),
            pltpu.SemaphoreType.DMA((experts,)),
            pltpu.SemaphoreType.DMA((experts,)),
            pltpu.SemaphoreType.DMA,
        ],
        compiler_params=pltpu.CompilerParams(
            collective_id=0, has_side_effects=True, vmem_limit_bytes=48 * 2**20
        ),
        cost_estimate=pl.CostEstimate(
            flops=2 * saved * width * depth, bytes_accessed=4 * depth * width, transcendentals=0
        ),
        name="reduce_grad",
    )(rows, grads, outgoing)


def product_kernel(
    n, experts, shard,
    weight_ref, tok_ref, back_ref,
    mate, held, prod, send_sem, recv_sem, mate_sem, back_send, back_recv, own_sem,
):
    index = lax.axis_index("dp")
    expert = lax.axis_index("expert")
    place, column = index // 2, lax.rem(index, 2)
    twin = place * 2 + 1 - column
    length = n // 2
    has_left = place > 0
    has_right = place < length - 1
    size = 128
    parts = shard // size
    count = tok_ref.shape[0] // experts
    half = length * shard

    def send(way, block, part, source):
        return pltpu.make_async_remote_copy(
            src_ref=source.at[pl.ds(part * size, size)],
            dst_ref=held.at[block, pl.ds(part * size, size)],
            send_sem=send_sem.at[(way + 1) // 2, block, part],
            recv_sem=recv_sem.at[block, part],
            device_id={"dp": jnp.clip(place + way, 0, length - 1) * 2 + column},
            device_id_type=MESH,
        )

    def swap():
        return pltpu.make_async_remote_copy(
            src_ref=tok_ref,
            dst_ref=mate,
            send_sem=mate_sem.at[0],
            recv_sem=mate_sem.at[1],
            device_id={"dp": twin},
            device_id_type=MESH,
        )

    def back_copy(side, other, here, there):
        peer = lax.rem(expert + other, experts)
        return pltpu.make_async_remote_copy(
            src_ref=prod.at[side, peer, :, here],
            dst_ref=back_ref.at[expert, :, there],
            send_sem=back_send.at[side, other],
            recv_sem=back_recv.at[side, other],
            device_id={"dp": twin if side else index, "expert": peer},
            device_id_type=MESH,
        )

    def multiply(side, weights, block, part):
        here = pl.ds(pl.multiple_of(block * shard + part * size, size), size)
        there = pl.ds(
            pl.multiple_of((block * 2 + column) * shard + part * size, size), size
        )
        out = lax.dot_general(
            (mate if side else tok_ref)[...],
            weights,
            (((1,), (1,)), ((), ())),
            preferred_element_type=jnp.float32,
        )
        prod[side, :, :, here] = out.astype(jnp.bfloat16).reshape(experts, count, size)
        for other in range(1 - side, experts):
            back_copy(side, other, here, there).start()
        if side == 0:
            pltpu.make_async_copy(
                prod.at[0, expert, :, here], back_ref.at[expert, :, there], own_sem
            ).start()

    barrier = pltpu.get_barrier_semaphore()
    for way, there in ((-1, has_left), (1, has_right)):

        @pl.when(there)
        def _():
            pl.semaphore_signal(
                barrier,
                inc=1,
                device_id={"dp": jnp.clip(place + way, 0, length - 1) * 2 + column},
                device_id_type=MESH,
            )

    for other in range(experts):
        peer = lax.rem(expert + other, experts)
        for to in (index, twin) if other else (twin,):
            pl.semaphore_signal(
                barrier, inc=1, device_id={"dp": to, "expert": peer}, device_id_type=MESH
            )
    pl.semaphore_wait(
        barrier, 2 * experts - 1 + has_left.astype(jnp.int32) + has_right.astype(jnp.int32)
    )

    swap().start()
    for part in range(parts):
        for way, there in ((-1, has_left), (1, has_right)):

            @pl.when(there)
            def _():
                send(way, place, part, weight_ref).start()

    for part in range(parts):
        multiply(0, weight_ref[pl.ds(part * size, size)], place, part)
    swap().wait()
    for part in range(parts):
        multiply(1, weight_ref[pl.ds(part * size, size)], place, part)

    def take(way, block, part, onward):
        send(way, block, part, weight_ref).wait_recv()

        @pl.when(onward)
        def _():
            send(way, block, part, held.at[block]).start()

        weights = held[block, pl.ds(part * size, size)]
        multiply(0, weights, block, part)
        multiply(1, weights, block, part)

    def step_on(step, _):
        for part in range(parts):
            before = place - 1 - step

            @pl.when(before >= 0)
            def _():
                take(1, before, part, has_right)

            after = place + 1 + step

            @pl.when(after < length)
            def _():
                take(-1, after, part, has_left)

        return 0

    lax.fori_loop(0, length - 1, step_on, 0)

    def drain(block, _):
        for part in range(parts):

            @pl.when((block <= place) & has_right)
            def _():
                send(1, block, part, weight_ref).wait_send()

            @pl.when((block >= place) & has_left)
            def _():
                send(-1, block, part, weight_ref).wait_send()

        return 0

    lax.fori_loop(0, length, drain, 0)
    whole = pl.ds(0, half)
    for side in (0, 1):
        for other in range(1 - side, experts):
            back_copy(side, other, whole, whole).wait()
    pltpu.make_async_copy(
        prod.at[0, expert], back_ref.at[expert, :, whole], own_sem
    ).wait()


def expert_product(n, experts, weights, tokens):
    shard, width = weights.shape
    depth = shard * n
    rows = tokens.shape[0]
    count = rows // experts
    parts = shard // 128
    return pl.pallas_call(
        functools.partial(product_kernel, n, experts, shard),
        out_shape=jax.ShapeDtypeStruct((experts, count, depth), jnp.bfloat16),
        in_specs=[pl.BlockSpec(memory_space=pltpu.VMEM)] * 2,
        out_specs=pl.BlockSpec(memory_space=pltpu.VMEM),
        scratch_shapes=[
            pltpu.VMEM((rows, width), jnp.bfloat16),
            pltpu.VMEM((n // 2, shard, width), jnp.bfloat16),
            pltpu.VMEM((2, experts, count, depth // 2), jnp.bfloat16),
            pltpu.SemaphoreType.DMA((2, n // 2, parts)),
            pltpu.SemaphoreType.DMA((n // 2, parts)),
            pltpu.SemaphoreType.DMA((2,)),
            pltpu.SemaphoreType.DMA((2, experts)),
            pltpu.SemaphoreType.DMA((2, experts)),
            pltpu.SemaphoreType.DMA,
        ],
        compiler_params=pltpu.CompilerParams(
            collective_id=1, has_side_effects=True, vmem_limit_bytes=48 * 2**20
        ),
        cost_estimate=pl.CostEstimate(
            flops=2 * rows * width * depth, bytes_accessed=4 * depth * width, transcendentals=0
        ),
        name="expert_product",
    )(weights, tokens)


def body(n, master, moment_one, moment_two, saved_rows, saved_grads, slot_rows, routes, gates):
    experts = lax.axis_size("expert")
    tok_count, top_count, width = slot_rows.shape
    capacity = tok_count * top_count * 5 // (4 * experts)
    capacity = -(-capacity // 16) * 16
    flat = routes.reshape(-1)
    turn = jnp.arange(flat.shape[0], dtype=jnp.int32)
    same = (flat[:, None] == flat[None, :]) & (turn[None, :] < turn[:, None])
    slot = flat * capacity + jnp.sum(same.astype(jnp.int32), axis=1)
    places = jnp.arange(experts * capacity, dtype=jnp.int32)
    pick = (places[:, None] == slot[None, :]).astype(jnp.bfloat16)
    outgoing = (
        jnp.dot(pick, slot_rows.reshape(-1, width), preferred_element_type=jnp.float32)
        .astype(jnp.bfloat16)
        .reshape(experts, capacity, width)
    )
    grad, received = reduce_grad(n, experts, saved_rows[0], saved_grads[0], outgoing)
    master_new, m_new, v_new = adam_update(master[0], moment_one[0], moment_two[0], grad)
    returned = expert_product(
        n, experts, master_new.astype(jnp.bfloat16), received.reshape(-1, width)
    ).reshape(experts * capacity, -1)
    slot = slot.reshape(tok_count, top_count)
    share = jnp.sum(
        jnp.where(slot[:, :, None] == places[None, None, :], gates[:, :, None], 0.0), axis=1
    )
    high = share.astype(jnp.bfloat16)
    low = (share - high.astype(jnp.float32)).astype(jnp.bfloat16)
    mixed = jnp.dot(high, returned, preferred_element_type=jnp.float32) + jnp.dot(
        low, returned, preferred_element_type=jnp.float32
    )
    return (master_new[None], m_new[None], v_new[None], mixed.astype(jnp.bfloat16))


def solution(mesh):
    placed = (
        P("expert", "dp", None),
        P("expert", "dp", None),
        P("expert", "dp", None),
        P("expert", "dp", None),
        P("expert", "dp", None),
        P(("dp", "expert"), None, None),
        P(("dp", "expert"), None),
        P(("dp", "expert"), None),
    )
    return jax.shard_map(
        functools.partial(body, mesh.shape["dp"]),
        mesh=mesh,
        in_specs=placed,
        out_specs=(
            P("expert", "dp", None),
            P("expert", "dp", None),
            P("expert", "dp", None),
            P(("dp", "expert"), None),
        ),
        check_vma=False,
    )
```

```python
import functools

import jax
import jax.numpy as jnp
from jax import lax
from jax.experimental import pallas as pl
from jax.experimental.pallas import tpu as pltpu
from jax.sharding import PartitionSpec as P

beta_one = 0.9
beta_two = 0.999
learn_rate = 0.002
tiny_eps = 1e-08
steps_done = 100.0

MESH = pl.DeviceIdType.MESH


def adam_update(master, moment_one, moment_two, grad):
    m_new = beta_one * moment_one + (1.0 - beta_one) * grad
    v_new = beta_two * moment_two + (1.0 - beta_two) * grad * grad
    fix_one = 1.0 - beta_one**steps_done
    fix_two = 1.0 - beta_two**steps_done
    step_size = m_new / fix_one / (jnp.sqrt(v_new / fix_two) + tiny_eps)
    return (master - learn_rate * step_size, m_new, v_new)


def lanes_of(shard):
    if shard % 512 == 0:
        part = shard // 4
        return ((1, 0, part), (-1, part, part), (1, 2 * part, part), (-1, 3 * part, part))
    return ((1, 0, shard),)


def ring_place(index, n):
    return jnp.where(lax.rem(index, 2) == 0, index // 2, (2 * n - 1 - index) // 2)


def ring_index(place, n):
    place = lax.rem(place + 2 * n, n)
    return jnp.where(place < n // 2, 2 * place, 2 * n - 1 - 2 * place)


def greet(n, experts, here, expert):
    barrier = pltpu.get_barrier_semaphore()
    for step in (1, -1):
        pl.semaphore_signal(
            barrier, inc=1, device_id={"dp": ring_index(here + step, n)}, device_id_type=MESH
        )
    for other in range(1, experts):
        pl.semaphore_signal(
            barrier,
            inc=1,
            device_id={"expert": lax.rem(expert + other, experts)},
            device_id_type=MESH,
        )
    pl.semaphore_wait(barrier, experts + 1)


def reduce_kernel(
    n, experts, shard,
    rows_ref, grads_ref, pick_ref, tok_ref, total_ref, got_ref,
    out_ref, first, slots, part, send_sem, recv_sem, tok_send, tok_recv, own_sem,
):
    here = ring_place(lax.axis_index("dp"), n)
    expert = lax.axis_index("expert")
    lanes = lanes_of(shard)

    def partial(place, low, size):
        at = pl.multiple_of(ring_index(place, n) * shard + low, size)
        return lax.dot_general(
            grads_ref[:, pl.ds(at, size)],
            rows_ref[...],
            (((0,), (0,)), ((), ())),
            preferred_element_type=jnp.float32,
        )

    def send(step, lane, source):
        way, low, size = lanes[lane]
        return pltpu.make_async_remote_copy(
            src_ref=source.at[pl.ds(low, size)],
            dst_ref=slots.at[step, pl.ds(low, size)],
            send_sem=send_sem.at[step, lane],
            recv_sem=recv_sem.at[step, lane],
            device_id={"dp": ring_index(here + way, n)},
            device_id_type=MESH,
        )

    def token_copy(other):
        peer = lax.rem(expert + other, experts)
        return pltpu.make_async_remote_copy(
            src_ref=out_ref.at[peer],
            dst_ref=got_ref.at[expert],
            send_sem=tok_send.at[other],
            recv_sem=tok_recv.at[other],
            device_id={"expert": peer},
            device_id_type=MESH,
        )

    greet(n, experts, here, expert)
    for lane, (way, low, size) in enumerate(lanes):
        first[pl.ds(low, size)] = partial(here - way, low, size).astype(jnp.bfloat16)
        send(0, lane, first).start()
    chosen = sum(
        jnp.dot(pick_ref[k], tok_ref[:, k, :], preferred_element_type=jnp.float32)
        for k in range(pick_ref.shape[0])
    )
    out_ref[...] = chosen.astype(jnp.bfloat16).reshape(out_ref.shape)
    for other in range(1, experts):
        token_copy(other).start()
    own = pltpu.make_async_copy(out_ref.at[expert], got_ref.at[expert], own_sem)
    own.start()

    def step_on(step, _):
        for lane, (way, low, size) in enumerate(lanes):
            part[pl.ds(low, size)] = partial(here - way * (2 + step), low, size)
            send(step, lane, first).wait_recv()
            slots[step, pl.ds(low, size)] = (
                slots[step, pl.ds(low, size)].astype(jnp.float32) + part[pl.ds(low, size)]
            ).astype(jnp.bfloat16)
            send(step + 1, lane, slots.at[step]).start()
        return 0

    lax.fori_loop(0, n - 2, step_on, 0)
    last = n - 2
    for lane, (way, low, size) in enumerate(lanes):
        part[pl.ds(low, size)] = partial(here, low, size)
    for lane, (way, low, size) in enumerate(lanes):
        send(last, lane, first).wait_recv()
        total_ref[pl.ds(low, size)] = (
            slots[last, pl.ds(low, size)].astype(jnp.float32) + part[pl.ds(low, size)]
        )

    def drain(step, _):
        for lane in range(len(lanes)):
            send(step, lane, first).wait_send()
        return 0

    lax.fori_loop(0, n - 1, drain, 0)
    for other in range(1, experts):
        token_copy(other).wait()
    own.wait()


def reduce_grad(n, experts, rows, grads, pick, tokens):
    saved, width = rows.shape
    depth = grads.shape[1]
    shard = depth // n
    lanes = len(lanes_of(shard))
    queue = (experts, pick.shape[1] // experts, width)
    return pl.pallas_call(
        functools.partial(reduce_kernel, n, experts, shard),
        out_shape=(
            jax.ShapeDtypeStruct((shard, width), jnp.float32),
            jax.ShapeDtypeStruct(queue, jnp.bfloat16),
        ),
        in_specs=[pl.BlockSpec(memory_space=pltpu.VMEM)] * 4,
        out_specs=(pl.BlockSpec(memory_space=pltpu.VMEM),) * 2,
        scratch_shapes=[
            pltpu.VMEM(queue, jnp.bfloat16),
            pltpu.VMEM((shard, width), jnp.bfloat16),
            pltpu.VMEM((n - 1, shard, width), jnp.bfloat16),
            pltpu.VMEM((shard, width), jnp.float32),
            pltpu.SemaphoreType.DMA((n - 1, lanes)),
            pltpu.SemaphoreType.DMA((n - 1, lanes)),
            pltpu.SemaphoreType.DMA((experts,)),
            pltpu.SemaphoreType.DMA((experts,)),
            pltpu.SemaphoreType.DMA,
        ],
        compiler_params=pltpu.CompilerParams(
            collective_id=0, has_side_effects=True, vmem_limit_bytes=48 * 2**20
        ),
        cost_estimate=pl.CostEstimate(
            flops=2 * saved * width * depth, bytes_accessed=4 * depth * width, transcendentals=0
        ),
        name="reduce_grad",
    )(rows, grads, pick, tokens)


def product_kernel(
    n, experts, shard,
    weight_ref, tok_ref, back_ref,
    mate, held, prod, send_sem, recv_sem, mate_sem, back_send, back_recv, own_sem,
):
    index = lax.axis_index("dp")
    expert = lax.axis_index("expert")
    place, column = index // 2, lax.rem(index, 2)
    twin = place * 2 + 1 - column
    length = n // 2
    has_left = place > 0
    has_right = place < length - 1
    size = 128
    parts = shard // size
    count = tok_ref.shape[0] // experts
    half = length * shard

    def send(way, block, part, source):
        return pltpu.make_async_remote_copy(
            src_ref=source.at[pl.ds(part * size, size)],
            dst_ref=held.at[block, pl.ds(part * size, size)],
            send_sem=send_sem.at[(way + 1) // 2, block, part],
            recv_sem=recv_sem.at[block, part],
            device_id={"dp": jnp.clip(place + way, 0, length - 1) * 2 + column},
            device_id_type=MESH,
        )

    def swap():
        return pltpu.make_async_remote_copy(
            src_ref=tok_ref,
            dst_ref=mate,
            send_sem=mate_sem.at[0],
            recv_sem=mate_sem.at[1],
            device_id={"dp": twin},
            device_id_type=MESH,
        )

    def back_copy(side, other, here, there):
        peer = lax.rem(expert + other, experts)
        return pltpu.make_async_remote_copy(
            src_ref=prod.at[side, peer, :, here],
            dst_ref=back_ref.at[expert, :, there],
            send_sem=back_send.at[side, other],
            recv_sem=back_recv.at[side, other],
            device_id={"dp": twin if side else index, "expert": peer},
            device_id_type=MESH,
        )

    def multiply(side, weights, block, part):
        here = pl.ds(pl.multiple_of(block * shard + part * size, size), size)
        there = pl.ds(
            pl.multiple_of((block * 2 + column) * shard + part * size, size), size
        )
        out = lax.dot_general(
            (mate if side else tok_ref)[...],
            weights,
            (((1,), (1,)), ((), ())),
            preferred_element_type=jnp.float32,
        )
        prod[side, :, :, here] = out.astype(jnp.bfloat16).reshape(experts, count, size)
        for other in range(1 - side, experts):
            back_copy(side, other, here, there).start()
        if side == 0:
            pltpu.make_async_copy(
                prod.at[0, expert, :, here], back_ref.at[expert, :, there], own_sem
            ).start()

    barrier = pltpu.get_barrier_semaphore()
    for way, there in ((-1, has_left), (1, has_right)):

        @pl.when(there)
        def _():
            pl.semaphore_signal(
                barrier,
                inc=1,
                device_id={"dp": jnp.clip(place + way, 0, length - 1) * 2 + column},
                device_id_type=MESH,
            )

    for other in range(experts):
        peer = lax.rem(expert + other, experts)
        for to in (index, twin) if other else (twin,):
            pl.semaphore_signal(
                barrier, inc=1, device_id={"dp": to, "expert": peer}, device_id_type=MESH
            )
    pl.semaphore_wait(
        barrier, 2 * experts - 1 + has_left.astype(jnp.int32) + has_right.astype(jnp.int32)
    )

    swap().start()
    for part in range(parts):
        for way, there in ((-1, has_left), (1, has_right)):

            @pl.when(there)
            def _():
                send(way, place, part, weight_ref).start()

    for part in range(parts):
        multiply(0, weight_ref[pl.ds(part * size, size)], place, part)
    swap().wait()
    for part in range(parts):
        multiply(1, weight_ref[pl.ds(part * size, size)], place, part)

    def take(way, block, part, onward):
        send(way, block, part, weight_ref).wait_recv()

        @pl.when(onward)
        def _():
            send(way, block, part, held.at[block]).start()

        weights = held[block, pl.ds(part * size, size)]
        multiply(0, weights, block, part)
        multiply(1, weights, block, part)

    def step_on(step, _):
        for part in range(parts):
            before = place - 1 - step

            @pl.when(before >= 0)
            def _():
                take(1, before, part, has_right)

            after = place + 1 + step

            @pl.when(after < length)
            def _():
                take(-1, after, part, has_left)

        return 0

    lax.fori_loop(0, length - 1, step_on, 0)

    def drain(block, _):
        for part in range(parts):

            @pl.when((block <= place) & has_right)
            def _():
                send(1, block, part, weight_ref).wait_send()

            @pl.when((block >= place) & has_left)
            def _():
                send(-1, block, part, weight_ref).wait_send()

        return 0

    lax.fori_loop(0, length, drain, 0)
    whole = pl.ds(0, half)
    for side in (0, 1):
        for other in range(1 - side, experts):
            back_copy(side, other, whole, whole).wait()
    pltpu.make_async_copy(
        prod.at[0, expert], back_ref.at[expert, :, whole], own_sem
    ).wait()


def expert_product(n, experts, weights, tokens):
    shard, width = weights.shape
    depth = shard * n
    rows = tokens.shape[0]
    count = rows // experts
    parts = shard // 128
    return pl.pallas_call(
        functools.partial(product_kernel, n, experts, shard),
        out_shape=jax.ShapeDtypeStruct((experts, count, depth), jnp.bfloat16),
        in_specs=[pl.BlockSpec(memory_space=pltpu.VMEM)] * 2,
        out_specs=pl.BlockSpec(memory_space=pltpu.VMEM),
        scratch_shapes=[
            pltpu.VMEM((rows, width), jnp.bfloat16),
            pltpu.VMEM((n // 2, shard, width), jnp.bfloat16),
            pltpu.VMEM((2, experts, count, depth // 2), jnp.bfloat16),
            pltpu.SemaphoreType.DMA((2, n // 2, parts)),
            pltpu.SemaphoreType.DMA((n // 2, parts)),
            pltpu.SemaphoreType.DMA((2,)),
            pltpu.SemaphoreType.DMA((2, experts)),
            pltpu.SemaphoreType.DMA((2, experts)),
            pltpu.SemaphoreType.DMA,
        ],
        compiler_params=pltpu.CompilerParams(
            collective_id=1, has_side_effects=True, vmem_limit_bytes=48 * 2**20
        ),
        cost_estimate=pl.CostEstimate(
            flops=2 * rows * width * depth, bytes_accessed=4 * depth * width, transcendentals=0
        ),
        name="expert_product",
    )(weights, tokens)


def body(n, master, moment_one, moment_two, saved_rows, saved_grads, slot_rows, routes, gates):
    experts = lax.axis_size("expert")
    tok_count, top_count, width = slot_rows.shape
    capacity = tok_count * top_count * 5 // (4 * experts)
    capacity = -(-capacity // 16) * 16
    flat = routes.reshape(-1)
    turn = jnp.arange(flat.shape[0], dtype=jnp.int32)
    same = (flat[:, None] == flat[None, :]) & (turn[None, :] < turn[:, None])
    slot = flat * capacity + jnp.sum(same.astype(jnp.int32), axis=1)
    places = jnp.arange(experts * capacity, dtype=jnp.int32)
    slot = slot.reshape(tok_count, top_count)
    pick = (places[None, :, None] == slot.T[:, None, :]).astype(jnp.bfloat16)
    grad, received = reduce_grad(n, experts, saved_rows[0], saved_grads[0], pick, slot_rows)
    master_new, m_new, v_new = adam_update(master[0], moment_one[0], moment_two[0], grad)
    returned = expert_product(
        n, experts, master_new.astype(jnp.bfloat16), received.reshape(-1, width)
    ).reshape(experts * capacity, -1)
    share = jnp.sum(
        jnp.where(slot[:, :, None] == places[None, None, :], gates[:, :, None], 0.0), axis=1
    )
    high = share.astype(jnp.bfloat16)
    low = (share - high.astype(jnp.float32)).astype(jnp.bfloat16)
    mixed = jnp.dot(high, returned, preferred_element_type=jnp.float32) + jnp.dot(
        low, returned, preferred_element_type=jnp.float32
    )
    return (master_new[None], m_new[None], v_new[None], mixed.astype(jnp.bfloat16))


def solution(mesh):
    placed = (
        P("expert", "dp", None),
        P("expert", "dp", None),
        P("expert", "dp", None),
        P("expert", "dp", None),
        P("expert", "dp", None),
        P(("dp", "expert"), None, None),
        P(("dp", "expert"), None),
        P(("dp", "expert"), None),
    )
    return jax.shard_map(
        functools.partial(body, mesh.shape["dp"]),
        mesh=mesh,
        in_specs=placed,
        out_specs=(
            P("expert", "dp", None),
            P("expert", "dp", None),
            P("expert", "dp", None),
            P(("dp", "expert"), None),
        ),
        check_vma=False,
    )
```
